256 devices in a mesh: ctx: 32 (over z_lo, y, core), head: 8 (over x, z_hi).
Axes of the slice: x: 4, y: 4, z: 8 (z_hi: 2, z_lo: 4; z = z_hi * 4 + z_lo), core: 2. Of those that a mesh axis runs over, the one named last changes fastest.
Arguments:
- queries: bfloat16 [8192, 5120], P('ctx', 'head'), may hold values from -45 to 45, as said below
- keys: bfloat16 [8192, 1024], P('ctx', 'head'), may hold values from -6 to 6
- values: bfloat16 [8192, 1024], P('ctx', 'head'), may hold values from -6 to 6
- grad_out: bfloat16 [8192, 5120], P('ctx', 'head'), may hold values from -6 to 6
- w_query: bfloat16 [5120, 5120], P(None, 'head'), may hold values from -0.078125 to 0.078125
Outputs:
- grad_input: bfloat16 [8192, 5120], P('ctx', 'head')
- grad_keys: bfloat16 [8192, 1024], P('ctx', 'head')
- grad_values: bfloat16 [8192, 1024], P('ctx', 'head')
The draws below stay inside these ranges and needn't reach their ends.
Inputs may be any that keep to these rules, and one draw needn't show every extreme that they name: queries of a few tokens may be large multiples of an earlier key.
All inputs are finite; a program needn't handle non-finite values.
Results may differ from the reference program's by a relative error of at most 0.025.
Values may be sent and summed in bfloat16 or wider, within the bound.
A program may use at most 128 MiB of HBM per device.

```python
import jax
import jax.numpy as jnp
from jax import lax

D = 5120
HQ = 40
KV = 8
HD = 128
TOKENS = 8192


def shared_keys(key):
    base_key = jax.random.fold_in(key, 5)
    return jnp.clip(jax.random.normal(base_key, (TOKENS, KV * HD), jnp.float32), -6.0, 6.0)


def draw_keys(key, part):
    return shared_keys(key).astype(jnp.bfloat16)


def draw_queries(key, part):
    key = jax.random.fold_in(key, 17)
    draws = jnp.clip(jax.random.normal(key, (TOKENS, HQ * HD), jnp.float32), -6.0, 6.0)
    return draws.astype(jnp.bfloat16)


def shard_levels(own_key, extent, cuts, smallest, top_value):
    def one(axis_at, parts):
        heights = jax.random.uniform(jax.random.fold_in(jax.random.fold_in(own_key, 6), axis_at), (parts,), jnp.float32, smallest / len(cuts), top_value / len(cuts))
        return jnp.repeat(jnp.exp(heights), extent[axis_at] // parts).reshape((-1,) + (1,) * (len(extent) - axis_at - 1))

    level = one(*cuts[0])
    for cut in cuts[1:]:
        level = level * one(*cut)
    return level


def centred(stream_key, shape, spread, bound, shards=(), kind=jnp.bfloat16):
    values = spread * jax.random.normal(stream_key, shape, jnp.float32)
    if shards:
        values = values * shard_levels(stream_key, shape, shards, -0.22, 0.18)
    return jnp.clip(values, -bound, bound).astype(kind)


def setup_inputs(seed: int = 0) -> dict:
    arg_keys = jax.random.split(jax.random.key(seed), 6)
    return {
        "queries": draw_queries(jax.random.fold_in(arg_keys[5], 71), 0),
        "keys": draw_keys(jax.random.fold_in(arg_keys[5], 71), 0),
        "values": centred(arg_keys[2], (TOKENS, KV * HD), 1.0, 6.0, ((0, 32), (1, 8))),
        "grad_out": centred(arg_keys[3], (TOKENS, HQ * HD), 1.0, 6.0, ((0, 32), (1, 8))),
        "w_query": centred(arg_keys[4], (D, HQ * HD), (HQ * HD) ** -0.5, 0.078125, ((1, 8),)),
    }


def reference(queries, keys, values, grad_out, w_query):
    group = HQ // KV
    scale = HD ** -0.5
    pos = jnp.arange(TOKENS, dtype=jnp.int32)
    causal = pos[None, :] <= pos[:, None]
    q_heads = queries.reshape(TOKENS, HQ, HD).transpose(1, 0, 2)
    o_heads = grad_out.reshape(TOKENS, HQ, HD).transpose(1, 0, 2)
    k_heads = keys.reshape(TOKENS, KV, HD).transpose(1, 0, 2)
    v_heads = values.reshape(TOKENS, KV, HD).transpose(1, 0, 2)

    def one_head(head):
        query = q_heads[head]
        dout = o_heads[head]
        key_h = k_heads[head // group]
        val_h = v_heads[head // group]
        scores = jnp.dot(query, key_h.T, preferred_element_type=jnp.float32) * scale
        scores = jnp.where(causal, scores, -jnp.inf)
        top = jnp.max(scores, axis=1, keepdims=True)
        lse = top + jnp.log(jnp.sum(jnp.exp(scores - top), axis=1, keepdims=True))
        probs = jnp.where(causal, jnp.exp(scores - lse), 0.0)
        dprobs = jnp.dot(dout, val_h.T, preferred_element_type=jnp.float32)
        delta = jnp.sum(probs * dprobs, axis=1, keepdims=True)
        probs_b = probs.astype(jnp.bfloat16)
        dscores = (probs * (dprobs - delta)).astype(jnp.bfloat16)
        grad_q = (jnp.dot(dscores, key_h, preferred_element_type=jnp.float32) * scale).astype(jnp.bfloat16)
        grad_k = jnp.dot(dscores.T, query, preferred_element_type=jnp.float32) * scale
        grad_v = jnp.dot(probs_b.T, dout, preferred_element_type=jnp.float32)
        return grad_q, grad_k, grad_v

    grad_q, grad_k, grad_v = lax.map(one_head, jnp.arange(HQ, dtype=jnp.int32))
    grad_k = grad_k.reshape(KV, group, TOKENS, HD).sum(axis=1)
    grad_v = grad_v.reshape(KV, group, TOKENS, HD).sum(axis=1)
    grad_keys = grad_k.transpose(1, 0, 2).reshape(TOKENS, KV * HD).astype(jnp.bfloat16)
    grad_values = grad_v.transpose(1, 0, 2).reshape(TOKENS, KV * HD).astype(jnp.bfloat16)
    q_flat = grad_q.transpose(1, 0, 2).reshape(TOKENS, HQ * HD)
    grad_input = lax.dot_general(q_flat, w_query, (((1,), (1,)), ((), ())), preferred_element_type=jnp.float32)
    return grad_input.astype(jnp.bfloat16), grad_keys, grad_values
```

```python
import functools

import jax
import jax.numpy as jnp
from jax import lax
from jax.experimental import pallas as pl
from jax.experimental.pallas import tpu as pltpu
from jax.sharding import PartitionSpec as P

HD = 128
B = 256
G = 5
R = G * B
NZ, NY, NK = 4, 4, 2
NX, NH = 4, 2
NB = NZ * NY * NK
ROW = NY * NK
COLS = G * HD
WIDE = NH * COLS
HALF = B // 2
SCALE = HD**-0.5
C = SCALE * 1.4426950408889634
NEG = -1e30
F32 = jnp.float32
BF = jnp.bfloat16
NT = (((1,), (1,)), ((), ()))
TN = (((0,), (0,)), ((), ()))
MESH = pl.DeviceIdType.MESH


def kernel(
    q_ref, k_ref, v_ref, o_ref, w_ref,
    gi_ref, gk_ref, gv_ref,
    kv, qa, oa, eb, db, ms, mr, lr, wr, dqt, dqb,
    ksta, ysta, zsta, zout, tot, s1, s2, hbuf,
    gz_s, gz_r, gy_s, gy_r, gk_s, gk_r,
    rk_s, rk_r, ry_s, ry_r, rz_s, rz_r,
    x1_s, x1_r, x2_s, x2_r, h_s, h_r, w_sem,
):
    ctx = lax.axis_index("ctx")
    head = lax.axis_index("head")
    k = lax.rem(ctx, NK)
    y = lax.rem(lax.div(ctx, NK), NY)
    z = lax.div(ctx, ROW)
    x = lax.div(head, NH)
    zh = lax.rem(head, NH)

    def at(zz, yy, kk):
        return ((zz * NY + yy) * NK + kk, head)

    def across(xx, hh):
        return (ctx, xx * NH + hh)

    def yp(d):
        return lax.rem(y + d, NY)

    def xp(d):
        return lax.rem(x + d, NX)

    sibling = at(z, y, 1 - k)
    up = at(jnp.minimum(z + 1, NZ - 1), y, k)
    down = at(jnp.maximum(z - 1, 0), y, k)

    def copy(src, dst, send, recv, to):
        return pltpu.make_async_remote_copy(
            src_ref=src, dst_ref=dst, send_sem=send, recv_sem=recv, device_id=to, device_id_type=MESH
        )

    def slot(row, yy, kk):
        return (row * NY + yy) * NK + kk

    kv[ctx, :, :HD] = k_ref[...]
    kv[ctx, :, HD:] = v_ref[...]
    for h in range(G):
        qa[h * B : (h + 1) * B, :] = q_ref[:, h * HD : (h + 1) * HD]
        oa[h * B : (h + 1) * B, :] = o_ref[:, h * HD : (h + 1) * HD]
    mr[...] = jnp.full_like(mr, NEG)
    lr[...] = jnp.zeros_like(lr)
    wr[...] = jnp.zeros_like(wr)

    barrier = pltpu.get_barrier_semaphore()

    def hello(to):
        pl.semaphore_signal(barrier, inc=1, device_id=to, device_id_type=MESH)

    hello(sibling)
    for d in range(1, NY):
        hello(at(z, yp(d), k))
    hello(across(xp(1), zh))
    hello(across(xp(NX - 1), zh))
    hello(across(x, 1 - zh))

    @pl.when(z < NZ - 1)
    def _():
        hello(up)

    @pl.when(z > 0)
    def _():
        hello(down)

    ends = jnp.where(z > 0, 1, 0) + jnp.where(z < NZ - 1, 1, 0)
    pl.semaphore_wait(barrier, NY + 3 + ends)

    def gather_z(s):
        b = kv.at[slot(z - s, y, k)]
        return copy(b, b, gz_s.at[s], gz_r.at[s + 1], up)

    def gather_z_in(s):
        b = kv.at[slot(z - s, y, k)]
        return copy(b, b, gz_s.at[s], gz_r.at[s], up)

    def gather_y(s, d):
        b = kv.at[slot(z - s, y, k)]
        return copy(b, b, gy_s.at[s, d - 1], gy_r.at[s, d - 1], at(z, yp(d), k))

    def gather_y_in(s, d):
        b = kv.at[slot(z - s, yp(NY - d), k)]
        return copy(b, b, gy_s.at[s, d - 1], gy_r.at[s, d - 1], at(z, yp(d), k))

    def gather_k(s, d):
        b = kv.at[slot(z - s, yp(NY - d), k)]
        return copy(b, b, gk_s.at[s, d], gk_r.at[s, d], sibling)

    def gather_k_in(s, d):
        b = kv.at[slot(z - s, yp(NY - d), 1 - k)]
        return copy(b, b, gk_s.at[s, d], gk_r.at[s, d], sibling)

    def gather_send(s):
        for d in (2, 1, 3):
            gather_y(s, d).start()

        @pl.when(z < NZ - 1)
        def _():
            gather_z(s).start()

        gather_k(s, 0).start()

    def gather_mid(s):
        for d in (1, 3, 2):
            gather_y_in(s, d).wait_recv()
            gather_k(s, d).start()

    def gather_end(s):
        for d in range(NY):
            gather_k_in(s, d).wait_recv()

    def first_block(j, masked):
        ks = pl.ds(pl.multiple_of(j * B, B), B)
        key = kv[j, :, :HD]
        val = kv[j, :, HD:]
        if masked:
            ok = lax.broadcasted_iota(jnp.int32, (B, B), 0) <= lax.broadcasted_iota(jnp.int32, (B, B), 1)
            ok3 = ok.reshape(B // 8, 8, B)
        for h in range(G):
            hs = slice(h * B, (h + 1) * B)
            s = lax.dot_general(key, qa[hs, :], NT, preferred_element_type=F32)
            t = lax.dot_general(val, oa[hs, :], NT, preferred_element_type=F32)
            if masked:
                s = jnp.where(ok, s, NEG)
            s3 = s.reshape(B // 8, 8, B)
            old = mr[:, hs]
            new = jnp.maximum(old, s3.max(0))
            e = jnp.exp2((s3 - new[None]) * C)
            if masked:
                e = jnp.where(ok3, e, 0.0)
            e_b = e.reshape(B, B).astype(BF)
            t_b = t.astype(BF)
            eb[ks, hs] = e_b
            db[ks, hs] = t_b
            e3 = e_b.astype(F32).reshape(B // 8, 8, B)
            t3 = t_b.astype(F32).reshape(B // 8, 8, B)
            f = jnp.exp2((old - new) * C)
            mr[:, hs] = new
            ms[j, :, hs] = new
            lr[:, hs] = lr[:, hs] * f + e3.sum(0)
            wr[:, hs] = wr[:, hs] * f + (e3 * t3).sum(0)

    def first_blocks(lo, hi):
        def body(j, _):
            first_block(j, False)
            return 0

        lax.fori_loop(lo, hi, body, 0)

    gather_send(0)
    first_block(ctx, True)
    gather_mid(0)
    gather_end(0)

    def first_row(s, _):
        base = (z - s) * ROW
        count = jnp.where(s == 0, ctx - z * ROW, ROW)
        half = lax.div(count, 2)

        @pl.when(s < z)
        def _():
            gather_z_in(s + 1).wait_recv()
            gather_send(s + 1)

        first_blocks(base, base + half)

        @pl.when(s < z)
        def _():
            gather_mid(s + 1)

        first_blocks(base + half, base + count)

        @pl.when(s < z)
        def _():
            gather_end(s + 1)

        return 0

    lax.fori_loop(0, z + 1, first_row, 0)

    def gather_sent(s, _):
        @pl.when(z < NZ - 1)
        def _():
            gather_z(s).wait_send()

        for d in range(1, NY):
            gather_y(s, d).wait_send()
        for d in range(NY):
            gather_k(s, d).wait_send()
        return 0

    lax.fori_loop(0, z + 1, gather_sent, 0)

    m8 = mr[...]
    top = m8.max(0, keepdims=True)
    f = jnp.exp2((m8 - top) * C)
    inv = 1.0 / (lr[...] * f).sum(0, keepdims=True)
    delta = (wr[...] * f).sum(0, keepdims=True) * inv
    mr[...] = jnp.broadcast_to(top, mr.shape)
    lr[...] = jnp.broadcast_to(inv, lr.shape)
    wr[...] = jnp.broadcast_to(delta, wr.shape)
    dqt[...] = jnp.zeros_like(dqt)

    def second_block(j, _):
        ks = pl.ds(pl.multiple_of(j * B, B), B)
        key = kv[j, :, :HD]
        dk = jnp.zeros((B, HD), F32)
        dv = jnp.zeros((B, HD), F32)
        for h in range(G):
            hs = slice(h * B, (h + 1) * B)
            f = jnp.exp2((ms[j, :, hs] - mr[:, hs]) * C) * lr[:, hs]
            p = eb[ks, hs].astype(F32).reshape(B // 8, 8, B) * f[None]
            ds = p * (db[ks, hs].astype(F32).reshape(B // 8, 8, B) - wr[:, hs][None])
            p_b = p.reshape(B, B).astype(BF)
            ds_b = ds.reshape(B, B).astype(BF)
            dv += jnp.dot(p_b, oa[hs, :], preferred_element_type=F32)
            dk += jnp.dot(ds_b, qa[hs, :], preferred_element_type=F32)
            dqt[:, hs] += lax.dot_general(key, ds_b, TN, preferred_element_type=F32)
        kv[j, :, :HD] = (dk * SCALE).astype(BF)
        kv[j, :, HD:] = dv.astype(BF)
        return 0

    def second_blocks(lo, hi):
        lax.fori_loop(lo, hi, second_block, 0)

    def sum_k(r, yy):
        return copy(kv.at[slot(r, yy, 1 - k)], ksta.at[r, yy], rk_s.at[r, yy], rk_r.at[r, yy], sibling)

    def sum_y(r, d):
        return copy(
            kv.at[slot(r, yp(d), k)], ysta.at[r, d - 1], ry_s.at[r, d - 1], ry_r.at[r, d - 1], at(z, yp(d), k)
        )

    def sum_z(r):
        return copy(zout.at[r], zsta.at[r], rz_s.at[r], rz_r.at[r], down)

    def sum_start(r):
        for yy in range(NY):
            sum_k(r, yy).start()

    def sum_mid(r):
        for yy in range(NY):
            sum_k(r, yy).wait_recv()
            b = slot(r, yy, k)
            kv[b] = (kv[b].astype(F32) + ksta[r, yy].astype(F32)).astype(BF)
        for d in (2, 1, 3):
            sum_y(r, d).start()

    def sum_row(r):
        t = kv[slot(r, y, k)].astype(F32)
        for d in range(1, NY):
            sum_y(r, d).wait_recv()
            t += ysta[r, d - 1].astype(F32)
        tot[r] = t

        @pl.when((z == NZ - 1) & (r < z))
        def _():
            zout[r] = t.astype(BF)
            sum_z(r).start()

    def fetch_w():
        return pltpu.make_async_copy(w_ref, eb.at[: NX * WIDE, :COLS], w_sem)

    def second_row(r, _):
        base = r * ROW
        count = jnp.where(r == z, ctx - z * ROW + 1, ROW)
        part = jnp.minimum(count, 2)

        @pl.when((r == z) & (z == NZ - 1))
        def _():
            fetch_w().start()

        second_blocks(base, base + part)

        @pl.when(r > 0)
        def _():
            sum_mid(r - 1)

        second_blocks(base + part, base + count)

        @pl.when(r > 0)
        def _():
            sum_row(r - 1)

        def clear(j, _):
            kv[j] = jnp.zeros((B, 2 * HD), BF)
            return 0

        lax.fori_loop(base + count, base + ROW, clear, 0)
        sum_start(r)
        return 0

    lax.fori_loop(0, z + 1, second_row, 0)

    @pl.when(z < NZ - 1)
    def _():
        fetch_w().start()

    for h in range(G):
        dqb[:, h * HD : (h + 1) * HD] = (dqt[:, h * B : (h + 1) * B] * SCALE).T.astype(BF)
    sum_mid(z)
    fetch_w().wait()

    def project(xx):
        out = lax.dot_general(
            dqb[...], eb[pl.ds(pl.multiple_of(xx * WIDE, WIDE), WIDE), :COLS], NT, preferred_element_type=F32
        )
        db[pl.ds(pl.multiple_of(xx * B, B), B), :] = out.astype(BF)

    def piece(xx, t, a):
        return db.at[pl.ds(pl.multiple_of(xx * B + t * HALF, HALF), HALF), a * COLS : (a + 1) * COLS]

    dx = (1, NX - 1)

    def two_away(t, a):
        return copy(piece(xp(2), t, a), s1.at[a, t], x1_s.at[a, t], x1_r.at[a, t], across(xp(dx[a]), zh))

    def next_to(t, way, a):
        return copy(
            piece(xp(dx[way]), t, a), s2.at[way, t, a], x2_s.at[way, t, a], x2_r.at[way, t, a],
            across(xp(dx[way]), zh),
        )

    def pass_on(t):
        for a in range(2):
            two_away(t, a).wait_recv()
            mine = piece(xp(dx[a]), t, a)
            mine[...] = (mine[...].astype(F32) + s1[a, t].astype(F32)).astype(BF)
            next_to(t, a, a).start()

    def z_half(t):
        return copy(hout(t), hbuf.at[t], h_s.at[t], h_r.at[t], across(x, 1 - zh))

    def hout(t):
        return db.at[pl.ds(NX * B + t * HALF, HALF), :COLS]

    def own_sum(t, a):
        out = piece(x, t, a)[...].astype(F32)
        for way in range(2):
            out += s2[way, t, a].astype(F32)
        return out

    project(xp(2))
    for t in range(2):
        for a in range(2):
            two_away(t, a).start()
    project(xp(1))
    next_to(0, 0, 1).start()
    project(xp(3))
    next_to(0, 1, 0).start()
    next_to(1, 0, 1).start()
    next_to(1, 1, 0).start()
    pass_on(0)
    project(x)
    pass_on(1)
    sum_row(z)

    for t in range(2):
        for way in range(2):
            for a in range(2):
                next_to(t, way, a).wait_recv()
        lo = own_sum(t, 0)
        hi = own_sum(t, 1)
        first = zh == 0
        hout(t)[...] = jnp.where(first, hi, lo).astype(BF)
        z_half(t).start()
        gi_ref[t * HALF : (t + 1) * HALF, :] = jnp.where(first, lo, hi).astype(BF)

    def chain(r, _):
        @pl.when(z < NZ - 1)
        def _():
            sum_z(r).wait_recv()
            tot[r] = tot[r] + zsta[r].astype(F32)

            @pl.when(r < z)
            def _():
                zout[r] = tot[r].astype(BF)
                sum_z(r).start()

        return 0

    lax.fori_loop(0, z + 1, chain, 0)
    gk_ref[...] = tot[z, :, :HD].astype(BF)
    gv_ref[...] = tot[z, :, HD:].astype(BF)

    for t in range(2):
        z_half(t).wait_recv()
        rows = slice(t * HALF, (t + 1) * HALF)
        gi_ref[rows, :] = (gi_ref[rows, :].astype(F32) + hbuf[t].astype(F32)).astype(BF)

    def sums_sent(r, _):
        for yy in range(NY):
            sum_k(r, yy).wait_send()
        for d in range(1, NY):
            sum_y(r, d).wait_send()

        @pl.when(r < z)
        def _():
            sum_z(r).wait_send()

        return 0

    lax.fori_loop(0, z + 1, sums_sent, 0)
    for t in range(2):
        for a in range(2):
            two_away(t, a).wait_send()
            for way in range(2):
                next_to(t, way, a).wait_send()
        z_half(t).wait_send()


def local(queries, keys, values, grad_out, w_query):
    dma = pltpu.SemaphoreType.DMA
    vm = pltpu.VMEM
    return pl.pallas_call(
        kernel,
        out_shape=(
            jax.ShapeDtypeStruct((B, COLS), BF),
            jax.ShapeDtypeStruct((B, HD), BF),
            jax.ShapeDtypeStruct((B, HD), BF),
        ),
        in_specs=[pl.BlockSpec(memory_space=pltpu.VMEM)] * 4 + [pl.BlockSpec(memory_space=pl.ANY)],
        out_specs=[pl.BlockSpec(memory_space=pltpu.VMEM)] * 3,
        scratch_shapes=[
            vm((NB, B, 2 * HD), BF),
            vm((R, HD), BF),
            vm((R, HD), BF),
            vm((NB * B, R), BF),
            vm((NB * B, R), BF),
            vm((NB, 8, R), F32),
            vm((8, R), F32),
            vm((8, R), F32),
            vm((8, R), F32),
            vm((HD, R), F32),
            vm((B, COLS), BF),
            vm((NZ, NY, B, 2 * HD), BF),
            vm((NZ, NY - 1, B, 2 * HD), BF),
            vm((NZ, B, 2 * HD), BF),
            vm((NZ, B, 2 * HD), BF),
            vm((NZ, B, 2 * HD), F32),
            vm((2, 2, HALF, COLS), BF),
            vm((2, 2, 2, HALF, COLS), BF),
            vm((2, HALF, COLS), BF),
            dma((NZ,)), dma((NZ + 1,)),
            dma((NZ, NY - 1)), dma((NZ, NY - 1)),
            dma((NZ, NY)), dma((NZ, NY)),
            dma((NZ, NY)), dma((NZ, NY)),
            dma((NZ, NY - 1)), dma((NZ, NY - 1)),
            dma((NZ,)), dma((NZ,)),
            dma((2, 2)), dma((2, 2)),
            dma((2, 2, 2)), dma((2, 2, 2)),
            dma((2,)), dma((2,)),
            dma(()),
        ],
        compiler_params=pltpu.CompilerParams(
            collective_id=0, has_side_effects=True, vmem_limit_bytes=62 * 1024 * 1024
        ),
    )(queries, keys, values, grad_out, w_query)


def solution(mesh):
    return jax.shard_map(
        local,
        mesh=mesh,
        in_specs=(
            P("ctx", "head"),
            P("ctx", "head"),
            P("ctx", "head"),
            P("ctx", "head"),
            P(None, "head"),
        ),
        out_specs=(P("ctx", "head"), P("ctx", "head"), P("ctx", "head")),
        check_vma=False,
    )
```

```python
import functools

import jax
import jax.numpy as jnp
from jax import lax
from jax.experimental import pallas as pl
from jax.experimental.pallas import tpu as pltpu
from jax.sharding import PartitionSpec as P

HD = 128
B = 256
G = 5
R = G * B
NZ, NY, NK = 4, 4, 2
NX, NH = 4, 2
NB = NZ * NY * NK
ROW = NY * NK
COLS = G * HD
WIDE = NH * COLS
HALF = B // 2
T = G * HALF
MID = NX * WIDE
SCALE = HD**-0.5
C = SCALE * 1.4426950408889634
NEG = -1e30
F32 = jnp.float32
BF = jnp.bfloat16
NT = (((1,), (1,)), ((), ()))
TN = (((0,), (0,)), ((), ()))
MESH = pl.DeviceIdType.MESH


def kernel(
    q_ref, k_ref, v_ref, o_ref, w_ref,
    gi_ref, gk_ref, gv_ref,
    kv, qa, oa, eb, db, ms, mr, lr, wr, dqt, dqb,
    ksta, ysta, osta, zsta, zout, tot, s1, s2, hbuf, tail,
    g0_s, g0_r, gz_s, gz_r, gy_s, gy_r, gk_s, gk_r,
    rk_s, rk_r, ry_s, ry_r, ro_s, ro_r, rz_s, rz_r,
    x1_s, x1_r, x2_s, x2_r, h_s, h_r, w_sem,
):
    ctx = lax.axis_index("ctx")
    head = lax.axis_index("head")
    k = lax.rem(ctx, NK)
    y = lax.rem(lax.div(ctx, NK), NY)
    z = lax.div(ctx, ROW)
    x = lax.div(head, NH)
    zh = lax.rem(head, NH)

    def at(zz, yy, kk):
        return ((zz * NY + yy) * NK + kk, head)

    def across(xx, hh):
        return (ctx, xx * NH + hh)

    def yp(d):
        return lax.rem(y + d, NY)

    def xp(d):
        return lax.rem(x + d, NX)

    sibling = at(z, y, 1 - k)
    above = jnp.minimum(z + 1, NZ - 1)
    below = jnp.maximum(z - 1, 0)

    def copy(src, dst, send, recv, to):
        return pltpu.make_async_remote_copy(
            src_ref=src, dst_ref=dst, send_sem=send, recv_sem=recv, device_id=to, device_id_type=MESH
        )

    def slot(row, yy, kk):
        return (row * NY + yy) * NK + kk

    kv[ctx, :, :HD] = k_ref[...]
    kv[ctx, :, HD:] = v_ref[...]
    for t in range(2):
        for h in range(G):
            rows = slice(t * T + h * HALF, t * T + (h + 1) * HALF)
            qa[rows, :] = q_ref[t * HALF : (t + 1) * HALF, h * HD : (h + 1) * HD]
            oa[rows, :] = o_ref[t * HALF : (t + 1) * HALF, h * HD : (h + 1) * HD]
    mr[...] = jnp.full_like(mr, NEG)
    lr[...] = jnp.zeros_like(lr)
    wr[...] = jnp.zeros_like(wr)

    barrier = pltpu.get_barrier_semaphore()

    def hello(to):
        pl.semaphore_signal(barrier, inc=1, device_id=to, device_id_type=MESH)

    hello(sibling)
    for d in range(1, NY):
        hello(at(z, yp(d), k))
    hello(across(xp(1), zh))
    hello(across(xp(NX - 1), zh))
    hello(across(x, 1 - zh))

    @pl.when(z < NZ - 1)
    def _():
        hello(at(above, y, k))
        hello(at(above, yp(NY - 1), k))

    @pl.when(z > 0)
    def _():
        hello(at(below, y, k))
        hello(at(below, yp(1), k))

    ends = jnp.where(z > 0, 2, 0) + jnp.where(z < NZ - 1, 2, 0)
    pl.semaphore_wait(barrier, NY + 3 + ends)

    def block(s, j, kk):
        return kv.at[slot(z - s, yp(j), kk)]

    def own_y(d):
        b = block(0, 0, k)
        return copy(b, b, g0_s.at[d - 1], g0_r.at[d - 1], at(z, yp(d), k))

    def own_y_in(d):
        b = block(0, NY - d, k)
        return copy(b, b, g0_s.at[d - 1], g0_r.at[d - 1], at(z, yp(d), k))

    def own_z(i):
        b = block(0, 0, k)
        return copy(b, b, gz_s.at[0, i], gz_r.at[1, i], at(above, yp(NY - i), k))

    def gather_z(s, i):
        b = block(s, i, k)
        return copy(b, b, gz_s.at[s, i], gz_r.at[s + 1, i], at(above, y, k))

    def gather_z_in(s, i):
        b = block(s, i, k)
        return copy(b, b, gz_s.at[s, i], gz_r.at[s, i], at(above, y, k))

    def gather_y(s, i):
        b = block(s, i, k)
        return copy(b, b, gy_s.at[s, i], gy_r.at[s, i], at(z, yp((1, NY - 1)[i]), k))

    def gather_y_in(s, i):
        b = block(s, (NY - 1, 2)[i], k)
        return copy(b, b, gy_s.at[s, i], gy_r.at[s, i], at(z, yp((1, NY - 1)[i]), k))

    def gather_k(s, j):
        b = block(s, j, k)
        return copy(b, b, gk_s.at[s, j], gk_r.at[s, j], sibling)

    def gather_k_in(s, j):
        b = block(s, j, 1 - k)
        return copy(b, b, gk_s.at[s, j], gk_r.at[s, j], sibling)

    def own_send():
        for d in (1, 2, 3):
            @pl.when(y + d < NY)
            def _(d=d):
                own_y(d).start()

        @pl.when(k == 0)
        def _():
            gather_k(0, 0).start()

        @pl.when(z < NZ - 1)
        def _():
            own_z(0).start()
            own_z(1).start()

    def gather_up(s):
        for i in range(2):
            gather_z_in(s, i).wait_recv()

            @pl.when(z < NZ - 1)
            def _(i=i):
                gather_z(s, i).start()

            gather_y(s, i).start()
            gather_k(s, i).start()

    def first_block(j, masked):
        ks = pl.ds(pl.multiple_of(j * B, B), B)
        key = kv[j, :, :HD]
        val = kv[j, :, HD:]
        if masked:
            key_at = lax.broadcasted_iota(jnp.int32, (B, B), 0)
            col = lax.broadcasted_iota(jnp.int32, (B, B), 1)
        for h in range(G):
            hs = slice(h * B, (h + 1) * B)
            s = lax.dot_general(key, qa[hs, :], NT, preferred_element_type=F32)
            t = lax.dot_general(val, oa[hs, :], NT, preferred_element_type=F32)
            if masked:
                row = col + h * B
                ok = key_at <= lax.rem(row, HALF) + jnp.where(row >= T, HALF, 0)
                ok3 = ok.reshape(B // 8, 8, B)
                s = jnp.where(ok, s, NEG)
            s3 = s.reshape(B // 8, 8, B)
            old = mr[:, hs]
            new = jnp.maximum(old, s3.max(0))
            e = jnp.exp2((s3 - new[None]) * C)
            if masked:
                e = jnp.where(ok3, e, 0.0)
            e_b = e.reshape(B, B).astype(BF)
            t_b = t.astype(BF)
            eb[ks, hs] = e_b
            db[ks, hs] = t_b
            e3 = e_b.astype(F32).reshape(B // 8, 8, B)
            t3 = t_b.astype(F32).reshape(B // 8, 8, B)
            f = jnp.exp2((old - new) * C)
            mr[:, hs] = new
            ms[j, :, hs] = new
            lr[:, hs] = lr[:, hs] * f + e3.sum(0)
            wr[:, hs] = wr[:, hs] * f + (e3 * t3).sum(0)

    def first_two(a, b):
        def body(n, _):
            first_block(jnp.where(n == 0, a, b), False)
            return 0

        lax.fori_loop(0, 2, body, 0)

    own_send()
    first_block(ctx, True)

    @pl.when(k == 1)
    def _():
        gather_k_in(0, 0).wait_recv()
        first_block(ctx - 1, False)

    def own_step(d, _):
        @pl.when(d <= y)
        def _():
            own_y_in(d).wait_recv()
            gather_k(0, NY - d).start()
            first_block(slot(z, y - d, k), False)

        @pl.when((d == 1) & (z > 0))
        def _():
            gather_up(1)

        @pl.when(d <= y)
        def _():
            gather_k_in(0, NY - d).wait_recv()
            first_block(slot(z, y - d, 1 - k), False)

        return 0

    lax.fori_loop(1, jnp.maximum(y, 1) + 1, own_step, 0)

    def first_row(s, _):
        r = z - s
        first_two(slot(r, y, k), slot(r, yp(1), k))
        gather_k_in(s, 0).wait_recv()
        gather_k_in(s, 1).wait_recv()
        first_two(slot(r, y, 1 - k), slot(r, yp(1), 1 - k))
        for i in range(2):
            gather_y_in(s, i).wait_recv()
            gather_k(s, (NY - 1, 2)[i]).start()
        first_two(slot(r, yp(3), k), slot(r, yp(2), k))

        @pl.when(s < z)
        def _():
            gather_up(s + 1)

        gather_k_in(s, 3).wait_recv()
        gather_k_in(s, 2).wait_recv()
        first_two(slot(r, yp(3), 1 - k), slot(r, yp(2), 1 - k))
        return 0

    lax.fori_loop(1, z + 1, first_row, 0)

    @pl.when(z < NZ - 1)
    def _():
        own_z(0).wait_send()
        own_z(1).wait_send()

    for d in range(1, NY):
        @pl.when(y + d < NY)
        def _(d=d):
            own_y(d).wait_send()

        @pl.when(y >= d)
        def _(d=d):
            gather_k(0, NY - d).wait_send()

    @pl.when(k == 0)
    def _():
        gather_k(0, 0).wait_send()

    def gather_sent(s, _):
        for i in range(2):
            @pl.when(z < NZ - 1)
            def _(i=i):
                gather_z(s, i).wait_send()

            gather_y(s, i).wait_send()
        for j in range(NY):
            gather_k(s, j).wait_send()
        return 0

    lax.fori_loop(1, z + 1, gather_sent, 0)

    m8 = mr[...]
    top = m8.max(0, keepdims=True)
    f = jnp.exp2((m8 - top) * C)
    inv = 1.0 / (lr[...] * f).sum(0, keepdims=True)
    delta = (wr[...] * f).sum(0, keepdims=True) * inv
    mr[...] = jnp.broadcast_to(top, mr.shape)
    lr[...] = jnp.broadcast_to(inv, lr.shape)
    wr[...] = jnp.broadcast_to(delta, wr.shape)
    dqt[...] = jnp.zeros_like(dqt)

    def second_blocks(half, lo, hi):
        cuts = ((0, 2 * HD), (2 * HD, 4 * HD), (4 * HD, 5 * HD))

        def body(j, _):
            ks = pl.ds(pl.multiple_of(j * B, B), B)
            key = kv[j, :, :HD]
            dk = jnp.zeros((B, HD), F32)
            dv = jnp.zeros((B, HD), F32)
            for start, stop in cuts:
                hs = slice(half * T + start, half * T + stop)
                f = jnp.exp2((ms[j, :, hs] - mr[:, hs]) * C) * lr[:, hs]
                p = eb[ks, hs].astype(F32).reshape(B // 8, 8, stop - start) * f[None]
                ds = p * (db[ks, hs].astype(F32).reshape(B // 8, 8, stop - start) - wr[:, hs][None])
                p_b = p.reshape(B, stop - start).astype(BF)
                ds_b = ds.reshape(B, stop - start).astype(BF)
                dv += jnp.dot(p_b, oa[hs, :], preferred_element_type=F32)
                dk += jnp.dot(ds_b, qa[hs, :], preferred_element_type=F32)
                dqt[:, hs] += lax.dot_general(key, ds_b, TN, preferred_element_type=F32)
            dk = dk * SCALE
            if half == 0:
                db[ks, :HD] = dk.astype(BF)
                db[ks, HD : 2 * HD] = dv.astype(BF)
            else:
                kv[j, :, :HD] = (dk + db[ks, :HD].astype(F32)).astype(BF)
                kv[j, :, HD:] = (dv + db[ks, HD : 2 * HD].astype(F32)).astype(BF)
            return 0

        lax.fori_loop(lo, hi, body, 0)

    def sum_k(r, j):
        return copy(kv.at[slot(r, yp(j), 1 - k)], ksta.at[r, j], rk_s.at[r, j], rk_r.at[r, j], sibling)

    def sum_y(r, i):
        b = kv.at[slot(r, yp((NY - 1, 2)[i]), k)]
        return copy(b, ysta.at[r, i], ry_s.at[r, i], ry_r.at[r, i], at(z, yp((NY - 1, 1)[i]), k))

    def sum_z(r, i):
        yy = y if i == 0 else jnp.where(z == r + 1, yp(1), y)
        return copy(zout.at[r, i], zsta.at[r, i], rz_s.at[r, i], rz_r.at[r, i], at(below, yy, k))

    def sum_own(d):
        return copy(
            kv.at[slot(z, yp(NY - d), k)], osta.at[d - 1], ro_s.at[d - 1], ro_r.at[d - 1], at(z, yp(NY - d), k)
        )

    def add_k(r, j):
        sum_k(r, j).wait_recv()
        b = slot(r, yp(j), k)
        kv[b] = (kv[b].astype(F32) + ksta[r, j].astype(F32)).astype(BF)

    def sum_start(r):
        for j in (3, 2, 0, 1):
            sum_k(r, j).start()

    def sum_mid(r):
        add_k(r, 3)
        sum_y(r, 0).start()
        add_k(r, 2)
        sum_y(r, 1).start()
        add_k(r, 0)
        add_k(r, 1)

    def sum_row(r):
        for i in range(2):
            sum_y(r, i).wait_recv()
            t = kv[slot(r, yp(i), k)].astype(F32) + ysta[r, i].astype(F32)
            tot[r, i] = t

            @pl.when(z == NZ - 1)
            def _(i=i, t=t):
                zout[r, i] = t.astype(BF)
                sum_z(r, i).start()

    def own_start():
        for d in range(1, NY):
            @pl.when(y >= d)
            def _(d=d):
                sum_k(z, NY - d).start()

        @pl.when(k == 1)
        def _():
            sum_k(z, 0).start()

    def own_add():
        for d in range(1, NY):
            @pl.when(y >= d)
            def _(d=d):
                add_k(z, NY - d)
                sum_own(d).start()

        @pl.when(k == 0)
        def _():
            add_k(z, 0)

    def own_row():
        tot[z, 0] = kv[slot(z, y, k)].astype(F32)
        for d in range(1, NY):
            @pl.when(y + d < NY)
            def _(d=d):
                sum_own(d).wait_recv()
                tot[z, 0] = tot[z, 0] + osta[d - 1].astype(F32)

    def chain(r, here):
        @pl.when((z < NZ - 1) & (r < z) & here)
        def _():
            for i in range(2):
                sum_z(r, i).wait_recv()
                zout[r, i] = (tot[r, i] + zsta[r, i].astype(F32)).astype(BF)
                sum_z(r, i).start()

    def fetch_w():
        return pltpu.make_async_copy(w_ref, eb.at[:MID, :COLS], w_sem)

    dx = (1, NX - 1)

    def rows_of(t, xx, a):
        return pl.ds(pl.multiple_of(MID + t * (NX * NH + 2) * HALF + (xx * NH + a) * HALF, HALF), HALF)

    def piece(t, xx, a):
        return eb.at[rows_of(t, xx, a), :COLS]

    def project(t, xx):
        for a in range(NH):
            w = eb[pl.ds(pl.multiple_of(xx * WIDE + a * COLS, COLS), COLS), :COLS]
            out = lax.dot_general(dqb[t], w, NT, preferred_element_type=F32)
            eb[rows_of(t, xx, a), :COLS] = out.astype(BF)

    def two_away(t, a):
        return copy(piece(t, xp(2), a), s1.at[t, a], x1_s.at[t, a], x1_r.at[t, a], across(xp(dx[a]), zh))

    def next_to(t, way, a):
        return copy(
            piece(t, xp(dx[way]), a), s2.at[t, way, a], x2_s.at[t, way, a], x2_r.at[t, way, a],
            across(xp(dx[way]), zh),
        )

    def pass_on(t):
        for a in range(2):
            two_away(t, a).wait_recv()
            mine = piece(t, xp(dx[a]), a)
            mine[...] = (mine[...].astype(F32) + s1[t, a].astype(F32)).astype(BF)
            next_to(t, a, a).start()

    def z_last(t):
        return copy(piece(t, NX, 0), hbuf.at[t], h_s.at[t], h_r.at[t], across(x, 1 - zh))

    def own_sum(t, a):
        out = piece(t, x, a)[...].astype(F32)
        for way in range(2):
            out += s2[t, way, a].astype(F32)
        return out

    def arrived(t):
        for way in range(2):
            for a in range(2):
                next_to(t, way, a).wait_recv()
        lo = own_sum(t, 0)
        hi = own_sum(t, 1)
        first = zh == 0
        out = piece(t, NX, 0)
        out[...] = jnp.where(first, hi, lo).astype(BF)
        z_last(t).start()
        tail[t] = jnp.where(first, lo, hi)

    def finish(t):
        z_last(t).wait_recv()
        gi_ref[t * HALF : (t + 1) * HALF, :] = (tail[t] + hbuf[t].astype(F32)).astype(BF)

    def round_x(t, beside):
        for h in range(G):
            cols = slice(t * T + h * HALF, t * T + (h + 1) * HALF)
            dqb[t, :, h * HD : (h + 1) * HD] = (dqt[:, cols] * SCALE).T.astype(BF)
        project(t, xp(2))
        for a in range(2):
            two_away(t, a).start()
        beside()
        project(t, xp(1))
        next_to(t, 0, 1).start()
        project(t, xp(3))
        next_to(t, 1, 0).start()
        project(t, x)

    def nothing():
        pass

    second_blocks(0, 0, z * ROW)

    @pl.when(z == NZ - 1)
    def _():
        fetch_w().start()

    second_blocks(0, z * ROW, ctx + 1)

    @pl.when(z < NZ - 1)
    def _():
        fetch_w().start()

    fetch_w().wait()
    round_x(0, nothing)

    def second_row(r, _):
        base = r * ROW
        count = jnp.where(r == z, ctx - z * ROW + 1, ROW)
        part = jnp.minimum(count, 2)
        second_blocks(1, base, base + part)

        @pl.when(r > 0)
        def _():
            sum_mid(r - 1)

        second_blocks(1, base + part, base + count)

        @pl.when(r > 1)
        def _():
            sum_row(r - 2)

        @pl.when(r < z)
        def _():
            sum_start(r)

        @pl.when(r == jnp.minimum(z, 1))
        def _():
            pass_on(0)

        return 0

    lax.fori_loop(0, z + 1, second_row, 0)
    own_start()
    round_x(1, own_add)

    @pl.when(z > 0)
    def _():
        sum_row(z - 1)

    arrived(0)
    chain(0, z == NZ - 2)
    pass_on(1)
    own_row()
    arrived(1)
    for r in range(NZ - 1):
        chain(r, (z < NZ - 2) | (r > 0))

    @pl.when(z < NZ - 1)
    def _():
        for i in range(2):
            sum_z(z, i).wait_recv()
            tot[z, 0] = tot[z, 0] + zsta[z, i].astype(F32)

    gk_ref[...] = tot[z, 0, :, :HD].astype(BF)
    gv_ref[...] = tot[z, 0, :, HD:].astype(BF)
    finish(0)
    finish(1)

    def sums_sent(r, _):
        for j in range(NY):
            sum_k(r, j).wait_send()
        for i in range(2):
            sum_y(r, i).wait_send()
            sum_z(r, i).wait_send()
        return 0

    lax.fori_loop(0, z, sums_sent, 0)
    for d in range(1, NY):
        @pl.when(y >= d)
        def _(d=d):
            sum_k(z, NY - d).wait_send()
            sum_own(d).wait_send()

    @pl.when(k == 1)
    def _():
        sum_k(z, 0).wait_send()

    for t in range(2):
        for a in range(2):
            two_away(t, a).wait_send()
            for way in range(2):
                next_to(t, way, a).wait_send()
        z_last(t).wait_send()


def hand_out(*refs):
    moves = [pltpu.make_async_copy(refs[i], refs[6 + i], refs[9].at[i]) for i in range(3)]
    outs = [pltpu.make_async_copy(refs[6 + i], refs[3 + i], refs[9].at[i]) for i in range(3)]
    for move in moves:
        move.start()
    for move, out in zip(moves, outs):
        move.wait()
        out.start()
    for out in outs:
        out.wait()


def local(queries, keys, values, grad_out, w_query):
    dma = pltpu.SemaphoreType.DMA
    vm = pltpu.VMEM
    shapes = (
        jax.ShapeDtypeStruct((B, COLS), BF),
        jax.ShapeDtypeStruct((B, HD), BF),
        jax.ShapeDtypeStruct((B, HD), BF),
    )
    outs = pl.pallas_call(
        kernel,
        out_shape=shapes,
        in_specs=[pl.BlockSpec(memory_space=pltpu.VMEM)] * 4 + [pl.BlockSpec(memory_space=pl.ANY)],
        out_specs=[pl.BlockSpec(memory_space=pltpu.VMEM)] * 3,
        scratch_shapes=[
            vm((NB, B, 2 * HD), BF),
            vm((R, HD), BF),
            vm((R, HD), BF),
            vm((NB * B, R), BF),
            vm((NB * B, R), BF),
            vm((NB, 8, R), F32),
            vm((8, R), F32),
            vm((8, R), F32),
            vm((8, R), F32),
            vm((HD, R), F32),
            vm((2, HALF, COLS), BF),
            vm((NZ, NY, B, 2 * HD), BF),
            vm((NZ - 1, 2, B, 2 * HD), BF),
            vm((NY - 1, B, 2 * HD), BF),
            vm((NZ - 1, 2, B, 2 * HD), BF),
            vm((NZ - 1, 2, B, 2 * HD), BF),
            vm((NZ, 2, B, 2 * HD), F32),
            vm((2, 2, HALF, COLS), BF),
            vm((2, 2, 2, HALF, COLS), BF),
            vm((2, HALF, COLS), BF),
            vm((2, HALF, COLS), F32),
            dma((NY - 1,)), dma((NY - 1,)),
            dma((NZ, 2)), dma((NZ, 2)),
            dma((NZ, 2)), dma((NZ, 2)),
            dma((NZ, NY)), dma((NZ, NY)),
            dma((NZ, NY)), dma((NZ, NY)),
            dma((NZ - 1, 2)), dma((NZ - 1, 2)),
            dma((NY - 1,)), dma((NY - 1,)),
            dma((NZ - 1, 2)), dma((NZ - 1, 2)),
            dma((2, 2)), dma((2, 2)),
            dma((2, 2, 2)), dma((2, 2, 2)),
            dma((2,)), dma((2,)),
            dma(()),
        ],
        compiler_params=pltpu.CompilerParams(
            collective_id=0, has_side_effects=True, vmem_limit_bytes=62 * 1024 * 1024
        ),
    )(queries, keys, values, grad_out, w_query)
    return pl.pallas_call(
        hand_out,
        out_shape=shapes,
        in_specs=[pl.BlockSpec(memory_space=pl.ANY)] * 3,
        out_specs=[pl.BlockSpec(memory_space=pl.ANY)] * 3,
        scratch_shapes=[vm(a.shape, a.dtype) for a in shapes] + [dma((3,))],
    )(*outs)


def solution(mesh):
    return jax.shard_map(
        local,
        mesh=mesh,
        in_specs=(
            P("ctx", "head"),
            P("ctx", "head"),
            P("ctx", "head"),
            P("ctx", "head"),
            P(None, "head"),
        ),
        out_specs=(P("ctx", "head"), P("ctx", "head"), P("ctx", "head")),
        check_vma=False,
    )
```

```python
import functools

import jax
import jax.numpy as jnp
from jax import lax
from jax.experimental import pallas as pl
from jax.experimental.pallas import tpu as pltpu
from jax.sharding import PartitionSpec as P

HD = 128
B = 256
G = 5
R = G * B
NZ, NY, NK = 4, 4, 2
NX, NH = 4, 2
NB = NZ * NY * NK
ROW = NY * NK
PAIR = NK * B
COLS = G * HD
WIDE = NH * COLS
HALF = B // 2
T = G * HALF
MID = NX * WIDE
SCALE = HD**-0.5
C = SCALE * 1.4426950408889634
NEG = -1e30
F32 = jnp.float32
BF = jnp.bfloat16
NT = (((1,), (1,)), ((), ()))
TN = (((0,), (0,)), ((), ()))
MESH = pl.DeviceIdType.MESH


def kernel(
    q_ref, k_ref, v_ref, o_ref, w_ref,
    gi_ref, gk_ref, gv_ref,
    kv, qa, oa, eb, db, ms, mr, lr, wr, dqt, dqb,
    ksta, ysta, osta, zsta, tot, s1, s2, hbuf,
    g0_s, g0_r, gz_s, gz_r, gy_s, gy_r, gk_s, gk_r,
    rk_s, rk_r, ry_s, ry_r, ro_s, ro_r, rz_s, rz_r,
    x1_s, x1_r, x2_s, x2_r, h_s, h_r, w_sem, in_sem,
):
    ctx = lax.axis_index("ctx")
    head = lax.axis_index("head")
    k = lax.rem(ctx, NK)
    y = lax.rem(lax.div(ctx, NK), NY)
    z = lax.div(ctx, ROW)
    x = lax.div(head, NH)
    zh = lax.rem(head, NH)

    def at(zz, yy, kk):
        return ((zz * NY + yy) * NK + kk, head)

    def across(xx, hh):
        return (ctx, xx * NH + hh)

    def yp(d):
        return lax.rem(y + d, NY)

    def xp(d):
        return lax.rem(x + d, NX)

    sibling = at(z, y, 1 - k)
    above = jnp.minimum(z + 1, NZ - 1)
    below = jnp.maximum(z - 1, 0)

    def copy(src, dst, send, recv, to):
        return pltpu.make_async_remote_copy(
            src_ref=src, dst_ref=dst, send_sem=send, recv_sem=recv, device_id=to, device_id_type=MESH
        )

    def slot(row, yy, kk):
        return (row * NY + yy) * NK + kk

    def load(src, dst, n):
        return pltpu.make_async_copy(src, dst, in_sem.at[n])

    own_loads = [load(k_ref, kv.at[ctx, :, :HD], 0), load(v_ref, kv.at[ctx, :, HD:], 1)]
    row_loads = []
    for t in range(2):
        for h in range(G):
            at_rows = pl.ds(t * HALF, HALF), pl.ds(h * HD, HD)
            to_rows = pl.ds(t * T + h * HALF, HALF)
            row_loads.append(load(q_ref.at[at_rows], qa.at[to_rows], 2 + len(row_loads)))
            row_loads.append(load(o_ref.at[at_rows], oa.at[to_rows], 2 + len(row_loads)))
    for one in own_loads + row_loads:
        one.start()
    mr[...] = jnp.full_like(mr, NEG)
    lr[...] = jnp.zeros_like(lr)
    wr[...] = jnp.zeros_like(wr)

    barrier = pltpu.get_barrier_semaphore()

    def hello(to):
        pl.semaphore_signal(barrier, inc=1, device_id=to, device_id_type=MESH)

    hello(sibling)
    for d in range(1, NY):
        hello(at(z, yp(d), k))
    hello(across(xp(1), zh))
    hello(across(xp(NX - 1), zh))
    hello(across(x, 1 - zh))

    @pl.when(z < NZ - 1)
    def _():
        hello(at(above, y, k))
        hello(at(above, yp(NY - 1), k))

    @pl.when(z > 0)
    def _():
        hello(at(below, y, k))
        hello(at(below, yp(1), k))

    ends = jnp.where(z > 0, 2, 0) + jnp.where(z < NZ - 1, 2, 0)
    pl.semaphore_wait(barrier, NY + 3 + ends)

    def block(s, j, kk):
        return kv.at[slot(z - s, yp(j), kk)]

    def own_y(d):
        b = block(0, 0, k)
        return copy(b, b, g0_s.at[d - 1], g0_r.at[d - 1], at(z, yp(d), k))

    def own_y_in(d):
        b = block(0, NY - d, k)
        return copy(b, b, g0_s.at[d - 1], g0_r.at[d - 1], at(z, yp(d), k))

    def own_z(i):
        b = block(0, 0, k)
        return copy(b, b, gz_s.at[0, i], gz_r.at[1, i], at(above, yp(NY - i), k))

    def gather_z(s, i):
        b = block(s, i, k)
        return copy(b, b, gz_s.at[s, i], gz_r.at[s + 1, i], at(above, y, k))

    def gather_z_in(s, i):
        b = block(s, i, k)
        return copy(b, b, gz_s.at[s, i], gz_r.at[s, i], at(above, y, k))

    def gather_y(s, i):
        b = block(s, i, k)
        return copy(b, b, gy_s.at[s, i], gy_r.at[s, i], at(z, yp((1, NY - 1)[i]), k))

    def gather_y_in(s, i):
        b = block(s, (NY - 1, 2)[i], k)
        return copy(b, b, gy_s.at[s, i], gy_r.at[s, i], at(z, yp((1, NY - 1)[i]), k))

    def gather_k(s, j):
        b = block(s, j, k)
        return copy(b, b, gk_s.at[s, j], gk_r.at[s, j], sibling)

    def gather_k_in(s, j):
        b = block(s, j, 1 - k)
        return copy(b, b, gk_s.at[s, j], gk_r.at[s, j], sibling)

    def own_send():
        for d in (1, 2, 3):
            @pl.when(y + d < NY)
            def _(d=d):
                own_y(d).start()

        gather_k(0, 0).start()

        @pl.when(z < NZ - 1)
        def _():
            own_z(0).start()
            own_z(1).start()

    def gather_up(s, i):
        gather_z_in(s, i).wait_recv()

        @pl.when(z < NZ - 1)
        def _():
            gather_z(s, i).start()

        gather_y(s, i).start()
        gather_k(s, i).start()

    def gather_over(s, i):
        gather_y_in(s, i).wait_recv()
        gather_k(s, (NY - 1, 2)[i]).start()

    def first_pair(n, masked):
        if masked:
            for lo in range(0, R, B):
                first_part(n, masked, lo, B)
        else:
            first_part(n, masked, 0, R)

    def first_part(n, masked, lo, W):
        hs = slice(lo, lo + W)
        ks = pl.ds(pl.multiple_of(n * PAIR, PAIR), PAIR)
        both = kv[pl.ds(n * NK, NK)].reshape(PAIR, 2 * HD)
        s = lax.dot_general(both[:, :HD], qa[hs, :], NT, preferred_element_type=F32)
        t = lax.dot_general(both[:, HD:], oa[hs, :], NT, preferred_element_type=F32)
        if masked:
            key_at = lax.broadcasted_iota(jnp.int32, (PAIR, W), 0)
            row = lax.broadcasted_iota(jnp.int32, (PAIR, W), 1) + lo
            token = lax.rem(row, HALF) + jnp.where(row >= T, HALF, 0) + k * B
            ok = key_at <= token
            s = jnp.where(ok, s, NEG)
        s3 = s.reshape(PAIR // 8, 8, W)
        old = mr[:, hs]
        new = jnp.maximum(old, s3.max(0))
        e = jnp.exp2((s3 - new[None]) * C)
        if masked:
            e = jnp.where(ok.reshape(PAIR // 8, 8, W), e, 0.0)
        t_b = t.astype(BF)
        eb[ks, hs] = e.reshape(PAIR, W).astype(BF)
        db[ks, hs] = t_b
        f = jnp.exp2((old - new) * C)
        mr[:, hs] = new
        ms[n, :, hs] = new
        lr[:, hs] = lr[:, hs] * f + e.sum(0)
        wr[:, hs] = wr[:, hs] * f + (e * t_b.astype(F32).reshape(PAIR // 8, 8, W)).sum(0)

    def pair(row, j):
        return row * NY + yp(j)

    for one in own_loads:
        one.wait()
    own_send()
    for one in row_loads:
        one.wait()
    gather_k_in(0, 0).wait_recv()
    first_pair(pair(z, 0), True)

    def own_in(d):
        @pl.when(y >= d)
        def _():
            own_y_in(d).wait_recv()
            gather_k(0, NY - d).start()

    own_in(1)

    @pl.when(z > 0)
    def _():
        gather_up(1, 0)

    own_in(2)

    def own_step(d, _):
        @pl.when(d <= y)
        def _():
            gather_k_in(0, NY - d).wait_recv()
            first_pair(z * NY + y - d, False)

        @pl.when(d == 1)
        def _():
            own_in(3)

        @pl.when((d == 1) & (z > 0))
        def _():
            gather_up(1, 1)

        return 0

    lax.fori_loop(1, jnp.maximum(y, 1) + 1, own_step, 0)

    ready = jnp.where(z < NZ - 1, 0, 2)

    def first_row(s, _):
        def step(n, _):
            j = jnp.where(n == 2, 3, jnp.where(n == 3, 2, n))

            @pl.when(n == 1)
            def _():
                gather_over(s, 0)

            @pl.when(n == 2)
            def _():
                gather_over(s, 1)

            @pl.when((n == ready) & (s < z))
            def _():
                gather_up(s + 1, 0)

            @pl.when((n == ready + 1) & (s < z))
            def _():
                gather_up(s + 1, 1)

            gather_k_in(s, j).wait_recv()
            first_pair(pair(z - s, j), False)
            return 0

        return lax.fori_loop(0, NY, step, 0)

    lax.fori_loop(1, z + 1, first_row, 0)

    @pl.when(z < NZ - 1)
    def _():
        own_z(0).wait_send()
        own_z(1).wait_send()

    for d in range(1, NY):
        @pl.when(y + d < NY)
        def _(d=d):
            own_y(d).wait_send()

        @pl.when(y >= d)
        def _(d=d):
            gather_k(0, NY - d).wait_send()

    gather_k(0, 0).wait_send()

    def gather_sent(s, _):
        for i in range(2):
            @pl.when(z < NZ - 1)
            def _(i=i):
                gather_z(s, i).wait_send()

            gather_y(s, i).wait_send()
        for j in range(NY):
            gather_k(s, j).wait_send()
        return 0

    lax.fori_loop(1, z + 1, gather_sent, 0)

    m8 = mr[...]
    top = m8.max(0, keepdims=True)
    f = jnp.exp2((m8 - top) * C)
    inv = 1.0 / (lr[...] * f).sum(0, keepdims=True)
    delta = (wr[...] * f).sum(0, keepdims=True) * inv
    mr[...] = jnp.broadcast_to(top, mr.shape)
    lr[...] = jnp.broadcast_to(inv, lr.shape)
    wr[...] = jnp.broadcast_to(delta, wr.shape)
    dqt[...] = jnp.zeros_like(dqt)

    def second_pairs(half, first, count):
        hs = slice(half * T, (half + 1) * T)
        rows = count * PAIR
        ks = pl.ds(pl.multiple_of(first * PAIR, PAIR), rows)
        blocks = pl.ds(first * NK, count * NK)
        p_b, ds_b = [], []
        for i in range(count):
            here = pl.ds(pl.multiple_of((first + i) * PAIR, PAIR), PAIR)
            f = jnp.exp2((ms[first + i, :, hs] - mr[:, hs]) * C) * lr[:, hs]
            p = eb[here, hs].astype(F32).reshape(PAIR // 8, 8, T) * f[None]
            ds = p * (db[here, hs].astype(F32).reshape(PAIR // 8, 8, T) - wr[:, hs][None])
            p_b.append(p.reshape(PAIR, T).astype(BF))
            ds_b.append(ds.reshape(PAIR, T).astype(BF))
        p_b = jnp.concatenate(p_b, axis=0)
        ds_b = jnp.concatenate(ds_b, axis=0)
        key = kv[blocks, :, :HD].reshape(rows, HD)
        dv = jnp.dot(p_b, oa[hs, :], preferred_element_type=F32)
        dk = jnp.dot(ds_b, qa[hs, :], preferred_element_type=F32) * SCALE
        dqt[:, hs] += lax.dot_general(key, ds_b, TN, preferred_element_type=F32)
        if half == 0:
            db[ks, :HD] = dk.astype(BF)
            db[ks, HD : 2 * HD] = dv.astype(BF)
        else:
            shape = (count * NK, B, HD)
            kv[blocks, :, :HD] = (dk + db[ks, :HD].astype(F32)).astype(BF).reshape(shape)
            kv[blocks, :, HD:] = (dv + db[ks, HD : 2 * HD].astype(F32)).astype(BF).reshape(shape)

    def second_own(half):
        def body(n, _):
            second_pairs(half, z * NY + n, 1)
            return 0

        lax.fori_loop(0, y + 1, body, 0)

    def sum_k(r, j):
        return copy(kv.at[slot(r, yp(j), 1 - k)], ksta.at[r, j], rk_s.at[r, j], rk_r.at[r, j], sibling)

    def sum_y(r, i):
        b = kv.at[slot(r, yp((NY - 1, 2)[i]), k)]
        return copy(b, ysta.at[r, i], ry_s.at[r, i], ry_r.at[r, i], at(z, yp((NY - 1, 1)[i]), k))

    def sum_z(r, i):
        yy = y if i == 0 else jnp.where(z == r + 1, yp(1), y)
        return copy(kv.at[slot(r, yp(i), k)], zsta.at[r, i], rz_s.at[r, i], rz_r.at[r, i], at(below, yy, k))

    def sum_own(d):
        return copy(
            kv.at[slot(z, yp(NY - d), k)], osta.at[d - 1], ro_s.at[d - 1], ro_r.at[d - 1], at(z, yp(NY - d), k)
        )

    def add_k(r, j):
        sum_k(r, j).wait_recv()
        b = slot(r, yp(j), k)
        kv[b] = (kv[b].astype(F32) + ksta[r, j].astype(F32)).astype(BF)

    def sum_start(r):
        for j in (3, 2, 0, 1):
            sum_k(r, j).start()

    def sum_mid(r):
        add_k(r, 3)
        sum_y(r, 0).start()
        add_k(r, 2)
        sum_y(r, 1).start()
        add_k(r, 0)
        add_k(r, 1)

    def sum_row(r):
        for i in range(2):
            sum_y(r, i).wait_recv()
            b = slot(r, yp(i), k)
            kv[b] = (kv[b].astype(F32) + ysta[r, i].astype(F32)).astype(BF)

            @pl.when(z == NZ - 1)
            def _(i=i):
                sum_z(r, i).start()

    def own_start():
        for d in range(1, NY):
            @pl.when(y >= d)
            def _(d=d):
                sum_k(z, NY - d).start()

        @pl.when(k == 1)
        def _():
            sum_k(z, 0).start()

    def own_add():
        for d in range(1, NY):
            @pl.when(y >= d)
            def _(d=d):
                add_k(z, NY - d)
                sum_own(d).start()

        @pl.when(k == 0)
        def _():
            add_k(z, 0)

    def own_row():
        tot[...] = kv[slot(z, y, k)].astype(F32)
        for d in range(1, NY):
            @pl.when(y + d < NY)
            def _(d=d):
                sum_own(d).wait_recv()
                tot[...] = tot[...] + osta[d - 1].astype(F32)

    def chain(r):
        @pl.when((z < NZ - 1) & (r < z))
        def _():
            for i in range(2):
                sum_z(r, i).wait_recv()
                b = slot(r, yp(i), k)
                kv[b] = (kv[b].astype(F32) + zsta[r, i].astype(F32)).astype(BF)
                sum_z(r, i).start()

    def fetch_w():
        return pltpu.make_async_copy(w_ref, eb.at[:MID, :COLS], w_sem)

    dx = (1, NX - 1)

    def rows_of(t, xx, a):
        return pl.ds(pl.multiple_of(MID + t * (NX * NH + 2) * HALF + (xx * NH + a) * HALF, HALF), HALF)

    def piece(t, xx, a):
        return eb.at[rows_of(t, xx, a), :COLS]

    def project(t, xx):
        for a in range(NH):
            w = eb[pl.ds(pl.multiple_of(xx * WIDE + a * COLS, COLS), COLS), :COLS]
            out = lax.dot_general(dqb[t], w, NT, preferred_element_type=F32)
            eb[rows_of(t, xx, a), :COLS] = out.astype(BF)

    def two_away(t, a):
        return copy(piece(t, xp(2), a), s1.at[t, a], x1_s.at[t, a], x1_r.at[t, a], across(xp(dx[a]), zh))

    def next_to(t, way, a):
        return copy(
            piece(t, xp(dx[way]), a), s2.at[t, way, a], x2_s.at[t, way, a], x2_r.at[t, way, a],
            across(xp(dx[way]), zh),
        )

    def pass_on(t):
        for a in range(2):
            two_away(t, a).wait_recv()
            mine = piece(t, xp(dx[a]), a)
            mine[...] = (mine[...].astype(F32) + s1[t, a].astype(F32)).astype(BF)
            next_to(t, a, a).start()

    def z_last(t):
        return copy(piece(t, NX, 0), hbuf.at[t], h_s.at[t], h_r.at[t], across(x, 1 - zh))

    def own_sum(t, a):
        out = piece(t, x, a)[...].astype(F32)
        for way in range(2):
            out += s2[t, way, a].astype(F32)
        return out

    def arrived(t):
        for way in range(2):
            for a in range(2):
                next_to(t, way, a).wait_recv()
        lo = own_sum(t, 0)
        hi = own_sum(t, 1)
        first = zh == 0
        out = piece(t, NX, 0)
        out[...] = jnp.where(first, hi, lo).astype(BF)
        z_last(t).start()
        dqt[:, t * T : (t + 1) * T] = jnp.where(first, lo, hi)

    def finish(t):
        z_last(t).wait_recv()
        gi_ref[t * HALF : (t + 1) * HALF, :] = (dqt[:, t * T : (t + 1) * T] + hbuf[t].astype(F32)).astype(BF)

    def round_x(t, beside):
        for h in range(G):
            cols = slice(t * T + h * HALF, t * T + (h + 1) * HALF)
            dqb[t, :, h * HD : (h + 1) * HD] = (dqt[:, cols] * SCALE).T.astype(BF)
        project(t, xp(2))
        for a in range(2):
            two_away(t, a).start()
        project(t, xp(1))
        next_to(t, 0, 1).start()
        beside()
        project(t, xp(3))
        next_to(t, 1, 0).start()
        project(t, x)

    def nothing():
        pass

    def second_two(n, _):
        second_pairs(0, 2 * n, 2)
        return 0

    lax.fori_loop(0, 2 * z, second_two, 0)

    @pl.when(z == NZ - 1)
    def _():
        fetch_w().start()

    second_own(0)

    @pl.when(z < NZ - 1)
    def _():
        fetch_w().start()

    fetch_w().wait()
    round_x(0, nothing)

    def second_row(r, _):
        def part(n, _):
            second_pairs(1, r * NY + 2 * n, 2)
            return 0

        lax.fori_loop(0, 2, part, 0)
        sum_start(r)

        @pl.when(r > 0)
        def _():
            sum_mid(r - 1)

        @pl.when(r == z - 1)
        def _():
            pass_on(0)

        return 0

    lax.fori_loop(0, z, second_row, 0)
    second_own(1)
    own_start()

    @pl.when(z == 0)
    def _():
        pass_on(0)

    @pl.when(z > 0)
    def _():
        sum_mid(z - 1)

    @pl.when(z > 1)
    def _():
        sum_row(0)

    def between():
        @pl.when(z > 2)
        def _():
            sum_row(1)

        own_add()

    round_x(1, between)

    @pl.when(z > 0)
    def _():
        sum_row(z - 1)

    arrived(0)
    pass_on(1)
    own_row()
    arrived(1)
    for r in range(NZ - 1):
        chain(r)

    @pl.when(z < NZ - 1)
    def _():
        for i in range(2):
            sum_z(z, i).wait_recv()
            tot[...] = tot[...] + zsta[z, i].astype(F32)

    gk_ref[...] = tot[:, :HD].astype(BF)
    gv_ref[...] = tot[:, HD:].astype(BF)
    finish(0)
    finish(1)

    def sums_sent(r, _):
        for j in range(NY):
            sum_k(r, j).wait_send()
        for i in range(2):
            sum_y(r, i).wait_send()
            sum_z(r, i).wait_send()
        return 0

    lax.fori_loop(0, z, sums_sent, 0)
    for d in range(1, NY):
        @pl.when(y >= d)
        def _(d=d):
            sum_k(z, NY - d).wait_send()
            sum_own(d).wait_send()

    @pl.when(k == 1)
    def _():
        sum_k(z, 0).wait_send()

    for t in range(2):
        for a in range(2):
            two_away(t, a).wait_send()
            for way in range(2):
                next_to(t, way, a).wait_send()
        z_last(t).wait_send()


def hand_out(*refs):
    moves = [pltpu.make_async_copy(refs[i], refs[6 + i], refs[9].at[i]) for i in range(3)]
    outs = [pltpu.make_async_copy(refs[6 + i], refs[3 + i], refs[9].at[i]) for i in range(3)]
    for move in moves:
        move.start()
    for move, out in zip(moves, outs):
        move.wait()
        out.start()
    for out in outs:
        out.wait()


def local(queries, keys, values, grad_out, w_query):
    dma = pltpu.SemaphoreType.DMA
    vm = pltpu.VMEM
    shapes = (
        jax.ShapeDtypeStruct((B, COLS), BF),
        jax.ShapeDtypeStruct((B, HD), BF),
        jax.ShapeDtypeStruct((B, HD), BF),
    )
    outs = pl.pallas_call(
        kernel,
        out_shape=shapes,
        in_specs=[pl.BlockSpec(memory_space=pl.ANY)] * 5,
        out_specs=[pl.BlockSpec(memory_space=pltpu.VMEM)] * 3,
        scratch_shapes=[
            vm((NB, B, 2 * HD), BF),
            vm((R, HD), BF),
            vm((R, HD), BF),
            vm((NB * B, R), BF),
            vm((NB * B, R), BF),
            vm((NB // NK, 8, R), F32),
            vm((8, R), F32),
            vm((8, R), F32),
            vm((8, R), F32),
            vm((HD, R), F32),
            vm((2, HALF, COLS), BF),
            vm((NZ, NY, B, 2 * HD), BF),
            vm((NZ - 1, 2, B, 2 * HD), BF),
            vm((NY - 1, B, 2 * HD), BF),
            vm((NZ - 1, 2, B, 2 * HD), BF),
            vm((B, 2 * HD), F32),
            vm((2, 2, HALF, COLS), BF),
            vm((2, 2, 2, HALF, COLS), BF),
            vm((2, HALF, COLS), BF),
            dma((NY - 1,)), dma((NY - 1,)),
            dma((NZ, 2)), dma((NZ, 2)),
            dma((NZ, 2)), dma((NZ, 2)),
            dma((NZ, NY)), dma((NZ, NY)),
            dma((NZ, NY)), dma((NZ, NY)),
            dma((NZ - 1, 2)), dma((NZ - 1, 2)),
            dma((NY - 1,)), dma((NY - 1,)),
            dma((NZ - 1, 2)), dma((NZ - 1, 2)),
            dma((2, 2)), dma((2, 2)),
            dma((2, 2, 2)), dma((2, 2, 2)),
            dma((2,)), dma((2,)),
            dma(()),
            dma((2 + 4 * G,)),
        ],
        compiler_params=pltpu.CompilerParams(
            collective_id=0, has_side_effects=True, vmem_limit_bytes=65000000
        ),
    )(queries, keys, values, grad_out, w_query)
    return pl.pallas_call(
        hand_out,
        out_shape=shapes,
        in_specs=[pl.BlockSpec(memory_space=pl.ANY)] * 3,
        out_specs=[pl.BlockSpec(memory_space=pl.ANY)] * 3,
        scratch_shapes=[vm(a.shape, a.dtype) for a in shapes] + [dma((3,))],
    )(*outs)


def solution(mesh):
    return jax.shard_map(
        local,
        mesh=mesh,
        in_specs=(
            P("ctx", "head"),
            P("ctx", "head"),
            P("ctx", "head"),
            P("ctx", "head"),
            P(None, "head"),
        ),
        out_specs=(P("ctx", "head"), P("ctx", "head"), P("ctx", "head")),
        check_vma=False,
    )
```

```python
import functools

import jax
import jax.numpy as jnp
from jax import lax
from jax.experimental import pallas as pl
from jax.experimental.pallas import tpu as pltpu
from jax.sharding import PartitionSpec as P

HD = 128
B = 256
G = 5
R = G * B
NZ, NY, NK = 4, 4, 2
NX, NH = 4, 2
NB = NZ * NY * NK
ROW = NY * NK
PAIR = NK * B
COLS = G * HD
WIDE = NH * COLS
HALF = B // 2
T = G * HALF
MID = NX * WIDE
SCALE = HD**-0.5
C = SCALE * 1.4426950408889634
NEG = -1e30
F32 = jnp.float32
BF = jnp.bfloat16
NT = (((1,), (1,)), ((), ()))
TN = (((0,), (0,)), ((), ()))
MESH = pl.DeviceIdType.MESH


def kernel(
    q_ref, k_ref, v_ref, o_ref, w_ref,
    gi_ref, gk_ref, gv_ref,
    kv, qa, oa, eb, db, ms, mr, lr, wr, dqt, dqb,
    ksta, ysta, osta, zsta, tot, s1, s2, hbuf,
    g0_s, g0_r, gz_s, gz_r, gy_s, gy_r, gk_s, gk_r,
    rk_s, rk_r, ry_s, ry_r, ro_s, ro_r, rz_s, rz_r,
    x1_s, x1_r, x2_s, x2_r, h_s, h_r, w_sem, in_sem,
):
    ctx = lax.axis_index("ctx")
    head = lax.axis_index("head")
    k = lax.rem(ctx, NK)
    y = lax.rem(lax.div(ctx, NK), NY)
    z = lax.div(ctx, ROW)
    x = lax.div(head, NH)
    zh = lax.rem(head, NH)

    def at(zz, yy, kk):
        return ((zz * NY + yy) * NK + kk, head)

    def across(xx, hh):
        return (ctx, xx * NH + hh)

    def yp(d):
        return lax.rem(y + d, NY)

    def xp(d):
        return lax.rem(x + d, NX)

    sibling = at(z, y, 1 - k)
    above = jnp.minimum(z + 1, NZ - 1)
    below = jnp.maximum(z - 1, 0)

    def copy(src, dst, send, recv, to):
        return pltpu.make_async_remote_copy(
            src_ref=src, dst_ref=dst, send_sem=send, recv_sem=recv, device_id=to, device_id_type=MESH
        )

    def slot(row, yy, kk):
        return (row * NY + yy) * NK + kk

    def load(src, dst, n):
        return pltpu.make_async_copy(src, dst, in_sem.at[n])

    own_loads = [load(k_ref, kv.at[ctx, :, :HD], 0), load(v_ref, kv.at[ctx, :, HD:], 1)]
    row_loads = []
    for t in range(2):
        for h in range(G):
            at_rows = pl.ds(t * HALF, HALF), pl.ds(h * HD, HD)
            to_rows = pl.ds(t * T + h * HALF, HALF)
            row_loads.append(load(q_ref.at[at_rows], qa.at[to_rows], 2 + len(row_loads)))
            row_loads.append(load(o_ref.at[at_rows], oa.at[to_rows], 2 + len(row_loads)))
    for one in own_loads + row_loads:
        one.start()
    mr[...] = jnp.full_like(mr, NEG)
    lr[...] = jnp.zeros_like(lr)
    wr[...] = jnp.zeros_like(wr)

    barrier = pltpu.get_barrier_semaphore()

    def hello(to):
        pl.semaphore_signal(barrier, inc=1, device_id=to, device_id_type=MESH)

    hello(sibling)
    for d in range(1, NY):
        hello(at(z, yp(d), k))
    hello(across(xp(1), zh))
    hello(across(xp(NX - 1), zh))
    hello(across(x, 1 - zh))

    @pl.when(z < NZ - 1)
    def _():
        hello(at(above, y, k))
        hello(at(above, yp(NY - 1), k))

    @pl.when(z > 0)
    def _():
        hello(at(below, y, k))
        hello(at(below, yp(1), k))

    ends = jnp.where(z > 0, 2, 0) + jnp.where(z < NZ - 1, 2, 0)
    pl.semaphore_wait(barrier, NY + 3 + ends)

    def block(s, j, kk):
        return kv.at[slot(z - s, yp(j), kk)]

    def own_y(d):
        b = block(0, 0, k)
        return copy(b, b, g0_s.at[d - 1], g0_r.at[d - 1], at(z, yp(d), k))

    def own_y_in(d):
        b = block(0, NY - d, k)
        return copy(b, b, g0_s.at[d - 1], g0_r.at[d - 1], at(z, yp(d), k))

    def own_z(i):
        b = block(0, 0, k)
        return copy(b, b, gz_s.at[0, i], gz_r.at[1, i], at(above, yp(NY - i), k))

    def gather_z(s, i):
        b = block(s, i, k)
        return copy(b, b, gz_s.at[s, i], gz_r.at[s + 1, i], at(above, y, k))

    def gather_z_in(s, i):
        b = block(s, i, k)
        return copy(b, b, gz_s.at[s, i], gz_r.at[s, i], at(above, y, k))

    def gather_y(s, i):
        b = block(s, i, k)
        return copy(b, b, gy_s.at[s, i], gy_r.at[s, i], at(z, yp((1, NY - 1)[i]), k))

    def gather_y_in(s, i):
        b = block(s, (NY - 1, 2)[i], k)
        return copy(b, b, gy_s.at[s, i], gy_r.at[s, i], at(z, yp((1, NY - 1)[i]), k))

    def gather_k(s, j):
        b = block(s, j, k)
        return copy(b, b, gk_s.at[s, j], gk_r.at[s, j], sibling)

    def gather_k_in(s, j):
        b = block(s, j, 1 - k)
        return copy(b, b, gk_s.at[s, j], gk_r.at[s, j], sibling)

    def own_send():
        for d in (1, 2, 3):
            @pl.when(y + d < NY)
            def _(d=d):
                own_y(d).start()

        gather_k(0, 0).start()

        @pl.when(z < NZ - 1)
        def _():
            own_z(0).start()
            own_z(1).start()

    def gather_up(s, i):
        gather_z_in(s, i).wait_recv()

        @pl.when(z < NZ - 1)
        def _():
            gather_z(s, i).start()

        gather_y(s, i).start()
        gather_k(s, i).start()

    def gather_over(s, i):
        gather_y_in(s, i).wait_recv()
        gather_k(s, (NY - 1, 2)[i]).start()

    def first_pair(n, masked):
        if masked:
            for lo in range(0, R, B):
                first_part(n, masked, lo, B)
        else:
            first_part(n, masked, 0, R)

    def first_part(n, masked, lo, W):
        hs = slice(lo, lo + W)
        ks = pl.ds(pl.multiple_of(n * PAIR, PAIR), PAIR)
        both = kv[pl.ds(n * NK, NK)].reshape(PAIR, 2 * HD)
        s = lax.dot_general(both[:, :HD], qa[hs, :], NT, preferred_element_type=F32)
        t = lax.dot_general(both[:, HD:], oa[hs, :], NT, preferred_element_type=F32)
        if masked:
            key_at = lax.broadcasted_iota(jnp.int32, (PAIR, W), 0)
            row = lax.broadcasted_iota(jnp.int32, (PAIR, W), 1) + lo
            token = lax.rem(row, HALF) + jnp.where(row >= T, HALF, 0) + k * B
            ok = key_at <= token
            s = jnp.where(ok, s, NEG)
        s3 = s.reshape(PAIR // 8, 8, W)
        old = mr[:, hs]
        new = jnp.maximum(old, s3.max(0))
        e = jnp.exp2((s3 - new[None]) * C)
        if masked:
            e = jnp.where(ok.reshape(PAIR // 8, 8, W), e, 0.0)
        t_b = t.astype(BF)
        eb[ks, hs] = e.reshape(PAIR, W).astype(BF)
        db[ks, hs] = t_b
        f = jnp.exp2((old - new) * C)
        mr[:, hs] = new
        ms[n, :, hs] = new
        lr[:, hs] = lr[:, hs] * f + e.sum(0)
        wr[:, hs] = wr[:, hs] * f + (e * t_b.astype(F32).reshape(PAIR // 8, 8, W)).sum(0)

    def pair(row, j):
        return row * NY + yp(j)

    for one in own_loads:
        one.wait()
    own_send()
    for one in row_loads:
        one.wait()
    gather_k_in(0, 0).wait_recv()
    first_pair(pair(z, 0), True)

    def own_in(d):
        @pl.when(y >= d)
        def _():
            own_y_in(d).wait_recv()
            gather_k(0, NY - d).start()

    own_in(1)

    @pl.when(z > 0)
    def _():
        gather_up(1, 0)

    own_in(2)

    def own_step(d, _):
        @pl.when(d <= y)
        def _():
            gather_k_in(0, NY - d).wait_recv()
            first_pair(z * NY + y - d, False)

        @pl.when(d == 1)
        def _():
            own_in(3)

        @pl.when((d == 1) & (z > 0))
        def _():
            gather_up(1, 1)

        return 0

    lax.fori_loop(1, jnp.maximum(y, 1) + 1, own_step, 0)

    ready = jnp.where(z < NZ - 1, 0, 2)

    def first_row(s, _):
        def step(n, _):
            j = jnp.where(n == 2, 3, jnp.where(n == 3, 2, n))

            @pl.when(n == 1)
            def _():
                gather_over(s, 0)

            @pl.when(n == 2)
            def _():
                gather_over(s, 1)

            @pl.when((n == ready) & (s < z))
            def _():
                gather_up(s + 1, 0)

            @pl.when((n == ready + 1) & (s < z))
            def _():
                gather_up(s + 1, 1)

            gather_k_in(s, j).wait_recv()
            first_pair(pair(z - s, j), False)
            return 0

        return lax.fori_loop(0, NY, step, 0)

    lax.fori_loop(1, z + 1, first_row, 0)

    @pl.when(z < NZ - 1)
    def _():
        own_z(0).wait_send()
        own_z(1).wait_send()

    for d in range(1, NY):
        @pl.when(y + d < NY)
        def _(d=d):
            own_y(d).wait_send()

        @pl.when(y >= d)
        def _(d=d):
            gather_k(0, NY - d).wait_send()

    gather_k(0, 0).wait_send()

    def gather_sent(s, _):
        for i in range(2):
            @pl.when(z < NZ - 1)
            def _(i=i):
                gather_z(s, i).wait_send()

            gather_y(s, i).wait_send()
        for j in range(NY):
            gather_k(s, j).wait_send()
        return 0

    lax.fori_loop(1, z + 1, gather_sent, 0)

    m8 = mr[...]
    top = m8.max(0, keepdims=True)
    f = jnp.exp2((m8 - top) * C)
    inv = 1.0 / (lr[...] * f).sum(0, keepdims=True)
    delta = (wr[...] * f).sum(0, keepdims=True) * inv
    mr[...] = jnp.broadcast_to(top, mr.shape)
    lr[...] = jnp.broadcast_to(inv, lr.shape)
    wr[...] = jnp.broadcast_to(delta, wr.shape)
    dqt[...] = jnp.zeros_like(dqt)

    def second_pairs(half, first, count):
        hs = slice(half * T, (half + 1) * T)
        rows = count * PAIR
        ks = pl.ds(pl.multiple_of(first * PAIR, PAIR), rows)
        blocks = pl.ds(first * NK, count * NK)
        p_b, ds_b = [], []
        for i in range(count):
            here = pl.ds(pl.multiple_of((first + i) * PAIR, PAIR), PAIR)
            f = jnp.exp2((ms[first + i, :, hs] - mr[:, hs]) * C) * lr[:, hs]
            p = eb[here, hs].astype(F32).reshape(PAIR // 8, 8, T) * f[None]
            ds = p * (db[here, hs].astype(F32).reshape(PAIR // 8, 8, T) - wr[:, hs][None])
            p_b.append(p.reshape(PAIR, T).astype(BF))
            ds_b.append(ds.reshape(PAIR, T).astype(BF))
        p_b = jnp.concatenate(p_b, axis=0)
        ds_b = jnp.concatenate(ds_b, axis=0)
        key = kv[blocks, :, :HD].reshape(rows, HD)
        dv = jnp.dot(p_b, oa[hs, :], preferred_element_type=F32)
        dk = jnp.dot(ds_b, qa[hs, :], preferred_element_type=F32) * SCALE
        dqt[:, hs] += lax.dot_general(key, ds_b, TN, preferred_element_type=F32)
        if half == 0:
            db[ks, :HD] = dk.astype(BF)
            db[ks, HD : 2 * HD] = dv.astype(BF)
        else:
            shape = (count * NK, B, HD)
            kv[blocks, :, :HD] = (dk + db[ks, :HD].astype(F32)).astype(BF).reshape(shape)
            kv[blocks, :, HD:] = (dv + db[ks, HD : 2 * HD].astype(F32)).astype(BF).reshape(shape)

    def second_own(half):
        def body(n, _):
            second_pairs(half, z * NY + n, 1)
            return 0

        lax.fori_loop(0, y + 1, body, 0)

    def sum_k(r, j):
        return copy(kv.at[slot(r, yp(j), 1 - k)], ksta.at[r, j], rk_s.at[r, j], rk_r.at[r, j], sibling)

    def sum_y(r, i):
        b = kv.at[slot(r, yp((NY - 1, 2)[i]), k)]
        return copy(b, ysta.at[r, i], ry_s.at[r, i], ry_r.at[r, i], at(z, yp((NY - 1, 1)[i]), k))

    def sum_z(r, i):
        yy = y if i == 0 else jnp.where(z == r + 1, yp(1), y)
        return copy(kv.at[slot(r, yp(i), k)], zsta.at[r, i], rz_s.at[r, i], rz_r.at[r, i], at(below, yy, k))

    def sum_own(d):
        return copy(
            kv.at[slot(z, yp(NY - d), k)], osta.at[d - 1], ro_s.at[d - 1], ro_r.at[d - 1], at(z, yp(NY - d), k)
        )

    def add_k(r, j):
        sum_k(r, j).wait_recv()
        b = slot(r, yp(j), k)
        kv[b] = (kv[b].astype(F32) + ksta[r, j].astype(F32)).astype(BF)

    def sum_start(r):
        for j in (3, 2, 0, 1):
            sum_k(r, j).start()

    def sum_mid(r):
        add_k(r, 3)
        sum_y(r, 0).start()
        add_k(r, 2)
        sum_y(r, 1).start()
        add_k(r, 0)
        add_k(r, 1)

    def sum_row(r):
        for i in range(2):
            sum_y(r, i).wait_recv()
            b = slot(r, yp(i), k)
            kv[b] = (kv[b].astype(F32) + ysta[r, i].astype(F32)).astype(BF)

            @pl.when(z == NZ - 1)
            def _(i=i):
                sum_z(r, i).start()

    def own_start():
        for d in range(1, NY):
            @pl.when(y >= d)
            def _(d=d):
                sum_k(z, NY - d).start()

        @pl.when(k == 1)
        def _():
            sum_k(z, 0).start()

    def own_add():
        for d in range(1, NY):
            @pl.when(y >= d)
            def _(d=d):
                add_k(z, NY - d)
                sum_own(d).start()

        @pl.when(k == 0)
        def _():
            add_k(z, 0)

    def own_row():
        tot[...] = kv[slot(z, y, k)].astype(F32)
        for d in range(1, NY):
            @pl.when(y + d < NY)
            def _(d=d):
                sum_own(d).wait_recv()
                tot[...] = tot[...] + osta[d - 1].astype(F32)

    def chain(r):
        @pl.when((z < NZ - 1) & (r < z))
        def _():
            for i in range(2):
                sum_z(r, i).wait_recv()
                b = slot(r, yp(i), k)
                kv[b] = (kv[b].astype(F32) + zsta[r, i].astype(F32)).astype(BF)
                sum_z(r, i).start()

    def fetch_w():
        return pltpu.make_async_copy(w_ref, eb.at[:MID, :COLS], w_sem)

    dx = (1, NX - 1)

    def rows_of(t, xx, a):
        return pl.ds(pl.multiple_of(MID + t * (NX * NH + 2) * HALF + (xx * NH + a) * HALF, HALF), HALF)

    def piece(t, xx, a):
        return eb.at[rows_of(t, xx, a), :COLS]

    def project(t, xx):
        for a in range(NH):
            w = eb[pl.ds(pl.multiple_of(xx * WIDE + a * COLS, COLS), COLS), :COLS]
            out = lax.dot_general(dqb[t], w, NT, preferred_element_type=F32)
            eb[rows_of(t, xx, a), :COLS] = out.astype(BF)

    def two_away(t, a):
        return copy(piece(t, xp(2), a), s1.at[t, a], x1_s.at[t, a], x1_r.at[t, a], across(xp(dx[a]), zh))

    def next_to(t, way, a):
        return copy(
            piece(t, xp(dx[way]), a), s2.at[t, way, a], x2_s.at[t, way, a], x2_r.at[t, way, a],
            across(xp(dx[way]), zh),
        )

    def pass_on(t):
        for a in range(2):
            two_away(t, a).wait_recv()
            mine = piece(t, xp(dx[a]), a)
            mine[...] = (mine[...].astype(F32) + s1[t, a].astype(F32)).astype(BF)
            next_to(t, a, a).start()

    def z_last(t):
        return copy(piece(t, NX, 0), hbuf.at[t], h_s.at[t], h_r.at[t], across(x, 1 - zh))

    def own_sum(t, a):
        out = piece(t, x, a)[...].astype(F32)
        for way in range(2):
            out += s2[t, way, a].astype(F32)
        return out

    def arrived(t):
        for way in range(2):
            for a in range(2):
                next_to(t, way, a).wait_recv()
        lo = own_sum(t, 0)
        hi = own_sum(t, 1)
        first = zh == 0
        out = piece(t, NX, 0)
        out[...] = jnp.where(first, hi, lo).astype(BF)
        z_last(t).start()
        dqt[:, t * T : (t + 1) * T] = jnp.where(first, lo, hi)

    def finish(t):
        z_last(t).wait_recv()
        gi_ref[t * HALF : (t + 1) * HALF, :] = (dqt[:, t * T : (t + 1) * T] + hbuf[t].astype(F32)).astype(BF)

    def round_x(t, beside):
        for h in range(G):
            cols = slice(t * T + h * HALF, t * T + (h + 1) * HALF)
            dqb[t, :, h * HD : (h + 1) * HD] = (dqt[:, cols] * SCALE).T.astype(BF)
        project(t, xp(2))
        for a in range(2):
            two_away(t, a).start()
        project(t, xp(1))
        next_to(t, 0, 1).start()
        beside()
        project(t, xp(3))
        next_to(t, 1, 0).start()
        project(t, x)

    def nothing():
        pass

    def second_two(n, _):
        second_pairs(0, 2 * n, 2)
        return 0

    lax.fori_loop(0, 2 * z, second_two, 0)

    @pl.when(z == NZ - 1)
    def _():
        fetch_w().start()

    second_own(0)

    @pl.when(z < NZ - 1)
    def _():
        fetch_w().start()

    fetch_w().wait()
    round_x(0, nothing)

    def second_row(r, _):
        def part(n, _):
            second_pairs(1, r * NY + 2 * n, 2)
            return 0

        lax.fori_loop(0, 2, part, 0)
        sum_start(r)

        @pl.when(r > 0)
        def _():
            sum_mid(r - 1)

        @pl.when(r > 1)
        def _():
            sum_row(r - 2)

        @pl.when(r == z - 1)
        def _():
            pass_on(0)

        return 0

    lax.fori_loop(0, z, second_row, 0)
    second_own(1)
    own_start()

    @pl.when(z == 0)
    def _():
        pass_on(0)

    @pl.when(z > 0)
    def _():
        sum_mid(z - 1)

    def between():
        @pl.when(z > 1)
        def _():
            sum_row(z - 2)

        own_add()

    round_x(1, between)

    @pl.when(z > 0)
    def _():
        sum_row(z - 1)

    arrived(0)
    pass_on(1)
    own_row()
    arrived(1)
    for r in range(NZ - 1):
        chain(r)

    @pl.when(z < NZ - 1)
    def _():
        for i in range(2):
            sum_z(z, i).wait_recv()
            tot[...] = tot[...] + zsta[z, i].astype(F32)

    gk_ref[...] = tot[:, :HD].astype(BF)
    gv_ref[...] = tot[:, HD:].astype(BF)
    finish(0)
    finish(1)

    def sums_sent(r, _):
        for j in range(NY):
            sum_k(r, j).wait_send()
        for i in range(2):
            sum_y(r, i).wait_send()
            sum_z(r, i).wait_send()
        return 0

    lax.fori_loop(0, z, sums_sent, 0)
    for d in range(1, NY):
        @pl.when(y >= d)
        def _(d=d):
            sum_k(z, NY - d).wait_send()
            sum_own(d).wait_send()

    @pl.when(k == 1)
    def _():
        sum_k(z, 0).wait_send()

    for t in range(2):
        for a in range(2):
            two_away(t, a).wait_send()
            for way in range(2):
                next_to(t, way, a).wait_send()
        z_last(t).wait_send()


def hand_out(*refs):
    moves = [pltpu.make_async_copy(refs[i], refs[6 + i], refs[9].at[i]) for i in range(3)]
    outs = [pltpu.make_async_copy(refs[6 + i], refs[3 + i], refs[9].at[i]) for i in range(3)]
    for move in moves:
        move.start()
    for move, out in zip(moves, outs):
        move.wait()
        out.start()
    for out in outs:
        out.wait()


def local(queries, keys, values, grad_out, w_query):
    dma = pltpu.SemaphoreType.DMA
    vm = pltpu.VMEM
    shapes = (
        jax.ShapeDtypeStruct((B, COLS), BF),
        jax.ShapeDtypeStruct((B, HD), BF),
        jax.ShapeDtypeStruct((B, HD), BF),
    )
    outs = pl.pallas_call(
        kernel,
        out_shape=shapes,
        in_specs=[pl.BlockSpec(memory_space=pl.ANY)] * 5,
        out_specs=[pl.BlockSpec(memory_space=pltpu.VMEM)] * 3,
        scratch_shapes=[
            vm((NB, B, 2 * HD), BF),
            vm((R, HD), BF),
            vm((R, HD), BF),
            vm((NB * B, R), BF),
            vm((NB * B, R), BF),
            vm((NB // NK, 8, R), F32),
            vm((8, R), F32),
            vm((8, R), F32),
            vm((8, R), F32),
            vm((HD, R), F32),
            vm((2, HALF, COLS), BF),
            vm((NZ, NY, B, 2 * HD), BF),
            vm((NZ - 1, 2, B, 2 * HD), BF),
            vm((NY - 1, B, 2 * HD), BF),
            vm((NZ - 1, 2, B, 2 * HD), BF),
            vm((B, 2 * HD), F32),
            vm((2, 2, HALF, COLS), BF),
            vm((2, 2, 2, HALF, COLS), BF),
            vm((2, HALF, COLS), BF),
            dma((NY - 1,)), dma((NY - 1,)),
            dma((NZ, 2)), dma((NZ, 2)),
            dma((NZ, 2)), dma((NZ, 2)),
            dma((NZ, NY)), dma((NZ, NY)),
            dma((NZ, NY)), dma((NZ, NY)),
            dma((NZ - 1, 2)), dma((NZ - 1, 2)),
            dma((NY - 1,)), dma((NY - 1,)),
            dma((NZ - 1, 2)), dma((NZ - 1, 2)),
            dma((2, 2)), dma((2, 2)),
            dma((2, 2, 2)), dma((2, 2, 2)),
            dma((2,)), dma((2,)),
            dma(()),
            dma((2 + 4 * G,)),
        ],
        compiler_params=pltpu.CompilerParams(
            collective_id=0, has_side_effects=True, vmem_limit_bytes=65000000
        ),
    )(queries, keys, values, grad_out, w_query)
    return pl.pallas_call(
        hand_out,
        out_shape=shapes,
        in_specs=[pl.BlockSpec(memory_space=pl.ANY)] * 3,
        out_specs=[pl.BlockSpec(memory_space=pl.ANY)] * 3,
        scratch_shapes=[vm(a.shape, a.dtype) for a in shapes] + [dma((3,))],
    )(*outs)


def solution(mesh):
    return jax.shard_map(
        local,
        mesh=mesh,
        in_specs=(
            P("ctx", "head"),
            P("ctx", "head"),
            P("ctx", "head"),
            P("ctx", "head"),
            P(None, "head"),
        ),
        out_specs=(P("ctx", "head"), P("ctx", "head"), P("ctx", "head")),
        check_vma=False,
    )
```
